32 devices in a mesh: ctx: 8 (over z, core), tp: 4 (over y, x).
Axes of the slice: x: 2, y: 2, z: 4, core: 2. Of those that a mesh axis runs over, the one named last changes fastest.
Arguments:
- queries: bfloat16 [3072, 16, 128], P('ctx', 'tp'), may hold values from -6 to 6
- key_tensor: bfloat16 [3072, 2, 128], P('ctx'), may hold values from -6 to 6
- value_tensor: bfloat16 [3072, 2, 128], P('ctx'), may hold values from -6 to 6
- attn_output: bfloat16 [3072, 16, 128], P('ctx', 'tp'), may hold values from -4 to 4
- logsumexp_rows: float32 [16, 3072], P('tp', 'ctx'), may hold values from 4 to 7
- grad_output: bfloat16 [3072, 8192], P(('ctx', 'tp')), may hold values from -6 to 6
- out_proj: bfloat16 [2048, 8192], P('tp'), may hold values from -0.0625 to 0.0625
- block_doc: int32 [24], replicated, may hold values from 0 to 5, never falling along the last dimension, each value on 1 to 12 neighbouring positions
Outputs:
- grad_query: bfloat16 [3072, 16, 128], P('ctx', 'tp')
- grad_key: bfloat16 [3072, 2, 128], P(('ctx', 'tp'))
- grad_value: bfloat16 [3072, 2, 128], P(('ctx', 'tp'))
The draws below stay inside these ranges and needn't reach their ends.
Inputs may be any that keep to these rules, and one draw needn't show every extreme that they name: `block_doc`: document ids never fall along the sequence; one document spans 1 to 12 blocks, and some document spans exactly 12 in every draw.
All inputs are finite; a program needn't handle non-finite values.
Results may differ from the reference program's by a relative error of at most 0.012.
Values may be sent and summed in bfloat16 or wider, within the bound.
No kernel may reach another device: no remote copies, remote signals or barrier semaphores. Data moves between devices by JAX's collectives and lax.ppermute only.
A program may use at most 64 MiB of HBM per device.

```python
import math
import jax
import jax.numpy as jnp
import numpy as np
from jax import lax

D = 8192
HEAD_SIZE = 128
QUERY_HEADS = 16
KEY_VALUE_HEADS = 2
TOKENS_PER_SHARD = 384
DOCBLK = 128
SPAN = 4
SEQUENCE_TOKENS = 3072
NBLK = 24
MOST_BLOCKS = 12


def block_scale(key, extent, shards, least, top_value):
    factor_of, own = 1.0, jax.random.fold_in(key, 6)
    for dim, blocks in shards:
        steps = jnp.exp(jax.random.uniform(jax.random.fold_in(own, dim), (blocks,), jnp.float32, least / len(shards), top_value / len(shards)))
        factor_of = factor_of * jnp.repeat(steps, extent[dim] // blocks).reshape([-1 if axis == dim else 1 for axis in range(len(extent))])
    return factor_of


def profile(number_of, total, bound, lean):
    loads = [(1 << 20) // math.isqrt(rank ** lean) + 1 for rank in range(2, number_of + 1)]
    surplus, holding = total - bound - (number_of - 1), [1] * (number_of - 1)
    while surplus > 0:
        free = [i for i in range(number_of - 1) if holding[i] < bound]
        whole, left = sum([loads[i] for i in free]), surplus
        for i in free:
            extra = min(bound - holding[i], max(1, left * loads[i] // whole), surplus)
            holding[i] = holding[i] + extra
            surplus = surplus - extra
    return np.array([bound] + holding)


def uneven_parts(stream_key, count, total, most, slope):
    if count == 2:
        one = jax.random.randint(stream_key, (), max(1, total - most), min(most, total - 1) + 1)
        return jnp.stack([one, total - one])
    tallies = jnp.asarray(profile(count, total, most, slope), jnp.int32)
    couples = (count - 1) // 2
    giver, receiver = tallies[1:1 + 2 * couples:2], tallies[2:2 + 2 * couples:2]
    room = jnp.minimum(giver - 1, most - receiver)
    shifted = jax.random.randint(jax.random.fold_in(stream_key, 1), (couples,), 0, 1 << 20) % (room + 1)
    tallies = tallies.at[1:1 + 2 * couples:2].set(giver - shifted).at[2:2 + 2 * couples:2].set(receiver + shifted)
    return tallies[jax.random.permutation(jax.random.fold_in(stream_key, 2), count)]


def normal_values(key, extent, spread, limit, shards=(), kind=jnp.bfloat16):
    result = jax.random.normal(key, extent, jnp.float32) * spread
    if len(shards) > 0:
        result = block_scale(key, extent, shards, -0.22, 0.18) * result
    return jnp.clip(result, min=-limit, max=limit).astype(kind)


def setup_inputs(seed: int = 0) -> dict:
    seeds = jax.random.split(jax.random.key(seed), 9)
    return {
        "queries": normal_values(seeds[0], (SEQUENCE_TOKENS, QUERY_HEADS, HEAD_SIZE), 1.0, 6.0, ((0, 8), (1, 4))),
        "key_tensor": normal_values(seeds[1], (SEQUENCE_TOKENS, KEY_VALUE_HEADS, HEAD_SIZE), 1.0, 6.0, ((0, 8),)),
        "value_tensor": normal_values(seeds[2], (SEQUENCE_TOKENS, KEY_VALUE_HEADS, HEAD_SIZE), 1.0, 6.0, ((0, 8),)),
        "attn_output": normal_values(seeds[3], (SEQUENCE_TOKENS, QUERY_HEADS, HEAD_SIZE), 0.3, 4.0, ((0, 8), (1, 4))),
        "logsumexp_rows": jnp.clip(4.0 + 3.0 * jax.random.uniform(seeds[4], (QUERY_HEADS, SEQUENCE_TOKENS), jnp.float32) ** block_scale(seeds[4], (QUERY_HEADS, SEQUENCE_TOKENS), ((0, 4), (1, 8)), -0.2, 0.2), 4.0, 7.0),
        "grad_output": normal_values(seeds[5], (SEQUENCE_TOKENS, D), 1.0, 6.0, ((0, 32),)),
        "out_proj": normal_values(seeds[6], (QUERY_HEADS * HEAD_SIZE, D), D ** -0.5, 0.0625, ((0, 4),)),
        "block_doc": jnp.searchsorted(jnp.cumsum(uneven_parts(seeds[7], NBLK // 4, NBLK, MOST_BLOCKS, 2)), jnp.arange(NBLK), side="right").astype(jnp.int32),
    }


def reference(queries, key_tensor, value_tensor, attn_output, logsumexp_rows, grad_output, out_proj, block_doc):
    single_float = jnp.float32
    query_group = QUERY_HEADS // KEY_VALUE_HEADS
    head_window = SPAN * TOKENS_PER_SHARD
    score_scale = HEAD_SIZE ** -0.5
    head_gradients = jnp.dot(grad_output, out_proj.T, preferred_element_type=single_float).astype(jnp.bfloat16)
    head_gradients = head_gradients.reshape(SEQUENCE_TOKENS, QUERY_HEADS, HEAD_SIZE)
    delta_terms = jnp.sum(head_gradients.astype(single_float) * attn_output.astype(single_float), axis=2)
    positions = jnp.arange(SEQUENCE_TOKENS, dtype=jnp.int32)
    token_doc = block_doc[positions // DOCBLK]
    doc_pad = jnp.concatenate([jnp.full((head_window,), -1, jnp.int32), token_doc])
    pos_pad = jnp.arange(SEQUENCE_TOKENS + head_window, dtype=jnp.int32) - head_window
    key_pad = jnp.pad(key_tensor.astype(single_float), ((head_window, 0), (0, 0), (0, 0)))
    value_pad = jnp.pad(value_tensor.astype(single_float), ((head_window, 0), (0, 0), (0, 0)))
    span_rows = head_window + TOKENS_PER_SHARD

    def one_block(carry, block_index):
        key_acc, value_acc = carry
        first_row_index = (block_index * TOKENS_PER_SHARD).astype(jnp.int32)
        query_block = lax.dynamic_slice_in_dim(queries, first_row_index, TOKENS_PER_SHARD, 0).astype(single_float).reshape(TOKENS_PER_SHARD, KEY_VALUE_HEADS, query_group, HEAD_SIZE)
        gradient_block = lax.dynamic_slice_in_dim(head_gradients, first_row_index, TOKENS_PER_SHARD, 0).astype(single_float).reshape(TOKENS_PER_SHARD, KEY_VALUE_HEADS, query_group, HEAD_SIZE)
        logsumexp_block = lax.dynamic_slice_in_dim(logsumexp_rows, first_row_index, TOKENS_PER_SHARD, 1).reshape(KEY_VALUE_HEADS, query_group, TOKENS_PER_SHARD)
        delta_block = lax.dynamic_slice_in_dim(delta_terms, first_row_index, TOKENS_PER_SHARD, 0).T.reshape(KEY_VALUE_HEADS, query_group, TOKENS_PER_SHARD)
        key_win = lax.dynamic_slice_in_dim(key_pad, first_row_index, span_rows, 0)
        value_win = lax.dynamic_slice_in_dim(value_pad, first_row_index, span_rows, 0)
        key_pos = lax.dynamic_slice_in_dim(pos_pad, first_row_index, span_rows, 0)
        key_doc = lax.dynamic_slice_in_dim(doc_pad, first_row_index, span_rows, 0)
        query_pos = first_row_index + jnp.arange(TOKENS_PER_SHARD, dtype=jnp.int32)
        query_doc = lax.dynamic_slice_in_dim(token_doc, first_row_index, TOKENS_PER_SHARD, 0)
        allowed = (query_doc[:, None] == key_doc[None, :]) & (key_pos[None, :] <= query_pos[:, None])
        scores = jnp.einsum("igzd,jgd->gzij", query_block, key_win) * score_scale
        prob_full = jnp.exp(jnp.where(allowed[None, None], scores - logsumexp_block[..., None], -1e30))
        dprobs = jnp.einsum("igzd,jgd->gzij", gradient_block, value_win)
        dscores = (prob_full * (dprobs - delta_block[..., None]) * score_scale).astype(jnp.bfloat16)
        dscores = lax.optimization_barrier(dscores).astype(single_float)
        prob_low = lax.optimization_barrier(prob_full.astype(jnp.bfloat16)).astype(single_float)
        grad_q_blk = jnp.einsum("gzij,jgd->igzd", dscores, key_win).reshape(TOKENS_PER_SHARD, QUERY_HEADS, HEAD_SIZE)
        grad_k_win = jnp.einsum("gzij,igzd->jgd", dscores, query_block)
        grad_v_win = jnp.einsum("gzij,igzd->jgd", prob_low, gradient_block)
        old_key = lax.dynamic_slice_in_dim(key_acc, first_row_index, span_rows, 0)
        old_value = lax.dynamic_slice_in_dim(value_acc, first_row_index, span_rows, 0)
        key_acc = lax.dynamic_update_slice_in_dim(key_acc, old_key + grad_k_win, first_row_index, 0)
        value_acc = lax.dynamic_update_slice_in_dim(value_acc, old_value + grad_v_win, first_row_index, 0)
        return (key_acc, value_acc), grad_q_blk.astype(jnp.bfloat16)

    empty_accumulator = jnp.zeros((SEQUENCE_TOKENS + head_window, KEY_VALUE_HEADS, HEAD_SIZE), single_float)
    block_ids = jnp.arange(SEQUENCE_TOKENS // TOKENS_PER_SHARD, dtype=jnp.int32)
    (key_acc, value_acc), grad_q_all = lax.scan(one_block, (empty_accumulator, empty_accumulator), block_ids)
    grad_query = grad_q_all.reshape(SEQUENCE_TOKENS, QUERY_HEADS, HEAD_SIZE)
    grad_key = key_acc[head_window:].astype(jnp.bfloat16)
    grad_value = value_acc[head_window:].astype(jnp.bfloat16)
    return (grad_query, grad_key, grad_value)
```

```python
import functools
from typing import NamedTuple

import jax
import jax.numpy as jnp
from jax import lax
from jax.experimental import pallas as pl
from jax.experimental.pallas import tpu as pltpu
from jax.sharding import PartitionSpec as P

DOCBLK = 128
RANKS_BACK = 4
TERMS = 3
LABELS = 16
FAR = 32768.0
COST = 1000
LOG2E = 1.4426950408889634
VMEM_LIMIT = 16 * 1024 * 1024


def dot_nt(a, b):
    return lax.dot_general(a, b, (((1,), (1,)), ((), ())), preferred_element_type=jnp.float32)


def dot_nn(a, b):
    return lax.dot_general(a, b, (((1,), (0,)), ((), ())), preferred_element_type=jnp.float32)


def split_terms(columns):
    rows = columns[0].shape[0]
    lane = lax.broadcasted_iota(jnp.int32, (rows, 128), 1)
    packed = jnp.zeros((rows, 128), jnp.float32)
    for h, rest in enumerate(columns):
        for i in range(TERMS):
            term = rest.astype(jnp.bfloat16).astype(jnp.float32)
            packed = jnp.where(lane == TERMS * h + i, term, packed)
            rest = rest - term
    return packed


def head_operand(full, head, heads):
    features = full[:, head * 128 : (head + 1) * 128]
    extra = full[:, heads * 128 :]
    lane = lax.broadcasted_iota(jnp.int32, extra.shape, 1)
    mine = ((lane >= TERMS * head) & (lane < TERMS * (head + 1))) | (lane >= TERMS * heads)
    return jnp.concatenate([features, jnp.where(mine, extra, jnp.zeros_like(extra))], axis=1)


def stack_heads(full, heads):
    return jnp.concatenate([head_operand(full, h, heads) for h in range(heads)], axis=0)


def row_places(peer, segments, chunk, shape, axis, copies):
    index = lax.broadcasted_iota(jnp.int32, shape, axis)
    place, start = index, 0
    for _ in range(copies):
        for j, low, size in segments:
            base = (peer ^ j) * chunk + low
            inside = (index >= start) & (index < start + size)
            place = jnp.where(inside, index - start + base, place)
            start += size
    return place


def prepare_kernel(
    plan, docs, query, attn, lse, key, value, query_out, attn_out, key_out, packed
):
    heads, kv_heads, chunk, scale = plan.heads, plan.kv_heads, plan.chunk, plan.scale
    tokens, width = query.shape
    rank, peer = lax.axis_index("ctx"), lax.axis_index("tp")
    blocks = tokens // DOCBLK
    pad = -heads % 8
    level = lse[...] * (1.0 / scale)
    if pad:
        level = jnp.concatenate([level, jnp.zeros((pad, tokens), jnp.float32)], axis=0)
    level = level.T
    terms = split_terms([level[:, h : h + 1] for h in range(heads)])
    lane = lax.broadcasted_iota(jnp.int32, (DOCBLK, 128), 1)
    labelled = (lane >= TERMS * heads) & (lane < TERMS * heads + LABELS)
    packed[:, :width] = query[...]
    for b in range(blocks):
        rows = slice(b * DOCBLK, (b + 1) * DOCBLK)
        label = TERMS * heads + lax.rem(docs[rank * blocks + b], LABELS)
        packed[rows, width:] = jnp.where(lane == label, 1.0, terms[rows]).astype(jnp.bfloat16)
        unlike = jnp.where(labelled & (lane != label), -FAR, 0.0)
        key_out[rows, 256:] = jnp.where(lane < TERMS * heads, -1.0, unlike).astype(jnp.bfloat16)
    group = peer // plan.sharing
    mine = pl.ds(pl.multiple_of(group * 128, 128), 128)
    key_out[:, :128] = key[:, mine]
    key_out[:, 128:256] = value[:, mine]
    start = 0
    for phase in plan.phases:
        for j, low, size in phase:
            rows = pl.ds(pl.multiple_of((peer ^ j) * chunk + low, 16), size)
            query_out[start : start + size, :] = packed[rows, :]
            attn_out[start : start + size, :] = attn[rows, :]
            start += size


def prepare(plan, docs, query, attn, lse, key, value):
    tokens, width = query.shape
    vmem = pl.BlockSpec(memory_space=pltpu.VMEM)
    return pl.pallas_call(
        functools.partial(prepare_kernel, plan),
        in_specs=[pl.BlockSpec(memory_space=pltpu.SMEM)] + [vmem] * 5,
        out_specs=[vmem] * 3,
        out_shape=[
            jax.ShapeDtypeStruct((tokens, width + 128), jnp.bfloat16),
            jax.ShapeDtypeStruct((tokens, width), jnp.bfloat16),
            jax.ShapeDtypeStruct((tokens, 384), jnp.bfloat16),
        ],
        scratch_shapes=[pltpu.VMEM((tokens, width + 128), jnp.bfloat16)],
        compiler_params=pltpu.CompilerParams(vmem_limit_bytes=VMEM_LIMIT),
        cost_estimate=pl.CostEstimate(flops=COST, bytes_accessed=0, transcendentals=0),
        name="prepare",
    )(docs, query, attn, lse, key, value)


def project_kernel(heads, parts, *refs):
    grads, weight, attn, out = refs[:parts], refs[parts], refs[parts + 1], refs[-1]
    width = weight.shape[0]
    rows = jnp.concatenate([g[...] for g in grads], axis=0) if parts > 1 else grads[0][...]
    deltas = []
    span = 2 * 128 if heads % 2 == 0 else 128
    for low in range(0, width, span):
        part = dot_nt(weight[low : low + span, :], rows).T.astype(jnp.bfloat16)
        out[:, low : low + span] = part
        product = part.astype(jnp.float32) * attn[:, low : low + span].astype(jnp.float32)
        for h in range(span // 128):
            deltas.append(jnp.sum(product[:, h * 128 : (h + 1) * 128], axis=1, keepdims=True))
    out[:, width:] = split_terms(deltas).astype(jnp.bfloat16)


def project(grads, weight, attn, heads):
    rows = sum(g.shape[0] for g in grads)
    width, depth = weight.shape
    vmem = pl.BlockSpec(memory_space=pltpu.VMEM)
    return pl.pallas_call(
        functools.partial(project_kernel, heads, len(grads)),
        in_specs=[vmem] * (len(grads) + 2),
        out_specs=vmem,
        out_shape=jax.ShapeDtypeStruct((rows, width + 128), jnp.bfloat16),
        compiler_params=pltpu.CompilerParams(vmem_limit_bytes=VMEM_LIMIT),
        cost_estimate=pl.CostEstimate(
            flops=COST, bytes_accessed=0, transcendentals=0
        ),
        name="project",
    )(*grads, weight, attn)


def reached(docs, rank, first_row, step, fits, blocks, back):
    if back:
        key_rank, query_rank = rank - step, rank
    else:
        key_rank, query_rank = rank, rank + step
    last = docs.shape[0] - 1
    key_doc = docs[jnp.clip(key_rank * blocks + blocks - 1, 0, last)]
    query_doc = docs[jnp.clip(query_rank * blocks + first_row // DOCBLK, 0, last)]
    return fits & (key_doc >= query_doc)


def first_row_of(plan, phase, peer):
    return functools.reduce(jnp.minimum, [(peer ^ j) * plan.chunk + low for j, low, _ in phase])


def put_rows(plan, peer, out, segments, source):
    at = 0
    for j, low, size in segments:
        place = pl.ds(pl.multiple_of((peer ^ j) * plan.chunk + low, 16), size)
        out[place, :] = source(at, size)
        at += size


def fetch(needed, pairs, sem):
    def copies(s):
        return [
            pltpu.make_async_copy(x, y, sem.at[len(pairs[s]) * s + i])
            for i, (x, y) in enumerate(pairs[s])
        ]

    for s, need in enumerate(needed):

        @pl.when(need)
        def _(s=s):
            for copy in copies(s):
                copy.start()

    def wait(s):
        for copy in copies(s):
            copy.wait()

    return wait


def behind(docs, rank, first_row, blocks):
    core = lax.rem(rank, 2)
    needed = []
    for s in range(6):
        step = 2 * s if s < 3 else 2 * (s - 3) + 2 * core - 1
        fits = (step >= 0) & (step <= RANKS_BACK) & (rank - step >= 0)
        needed.append(reached(docs, rank, first_row, step, fits, blocks, True))
    return needed


def early_kernel(plan, parts, docs, *refs):
    heads, scale, phase = plan.heads, plan.scale, plan.phases[0]
    keys, qx, oxs = refs[:6], refs[6], refs[7 : 7 + parts]
    query_out, own_out, other_out, turned, block, sem = refs[7 + parts :]
    rows, tokens = query_out.shape[0], keys[0].shape[0]
    rank, peer = lax.axis_index("ctx"), lax.axis_index("tp")
    needed = behind(docs, rank, first_row_of(plan, phase, peer), plan.blocks)
    wait = fetch(needed, [[(keys[s], block.at[s])] for s in range(6)], sem)
    turned[...] = jnp.zeros_like(turned)
    queries = stack_heads(qx[:rows, :], heads)
    grads = stack_heads(jnp.concatenate([x[...] for x in oxs], axis=0), heads)
    for s in range(6):
        out = own_out.at[s] if s < 3 else other_out.at[s - 3]

        @pl.when(needed[s])
        def _(s=s, out=out):
            wait(s)
            key, value, extra = block[s, :, :128], block[s, :, 128:256], block[s, :, 256:]
            scores = dot_nt(jnp.concatenate([key, extra], axis=1), queries)
            if s == 0:
                place = lax.broadcasted_iota(jnp.int32, scores.shape, 0)
                seats = row_places(peer, phase, plan.chunk, (1, heads * rows), 1, heads)
                scores = jnp.where(place <= seats, scores, -FAR)
            probs = jnp.exp2(scores * (scale * LOG2E))
            dprobs = dot_nt(jnp.concatenate([value, extra], axis=1), grads)
            dscores = (probs * dprobs).astype(jnp.bfloat16)
            turned[...] += dot_nn(key.T, dscores)
            out[:, :128] = (dot_nn(dscores, queries[:, :128]) * scale).astype(out.dtype)
            out[:, 128:] = dot_nn(probs.astype(jnp.bfloat16), grads[:, :128]).astype(out.dtype)

        @pl.when(jnp.logical_not(needed[s]))
        def _(out=out):
            out[...] = jnp.zeros(out.shape, out.dtype)

    for h in range(heads):
        query_out[:, h * 128 : (h + 1) * 128] = (
            (turned[:, h * rows : (h + 1) * rows] * scale).T.astype(jnp.bfloat16)
        )


def early_gradients(plan, docs, keys, qx, oxs):
    rows, tokens = sum(x.shape[0] for x in oxs), keys[0].shape[0]
    vmem, any_place = pl.BlockSpec(memory_space=pltpu.VMEM), pl.BlockSpec(memory_space=pl.ANY)
    return pl.pallas_call(
        functools.partial(early_kernel, plan, len(oxs)),
        in_specs=[pl.BlockSpec(memory_space=pltpu.SMEM)] + [any_place] * 6 + [vmem] * (1 + len(oxs)),
        out_specs=[vmem] * 3,
        out_shape=[
            jax.ShapeDtypeStruct((rows, plan.heads * 128), jnp.bfloat16),
            jax.ShapeDtypeStruct((3, tokens, 256), jnp.bfloat16),
            jax.ShapeDtypeStruct((3, tokens, 256), jnp.bfloat16),
        ],
        scratch_shapes=[
            pltpu.VMEM((128, plan.heads * rows), jnp.float32),
            pltpu.VMEM((6, *keys[0].shape), jnp.bfloat16),
            pltpu.SemaphoreType.DMA((6,)),
        ],
        compiler_params=pltpu.CompilerParams(vmem_limit_bytes=VMEM_LIMIT),
        cost_estimate=pl.CostEstimate(flops=COST, bytes_accessed=0, transcendentals=0),
        name="early_gradients",
    )(docs, *keys, qx, *oxs)


def query_kernel(plan, number, before, docs, *refs):
    heads, scale, phase = plan.heads, plan.scale, plan.phases[number]
    start = sum(size for p in plan.phases[1:number] for _, _, size in p)
    keys, (qx, ox), done = refs[:6], refs[6:8], refs[8 : 8 + before]
    out, total, block, sem = refs[8 + before :]
    rows = ox.shape[0]
    rank, peer = lax.axis_index("ctx"), lax.axis_index("tp")
    needed = behind(docs, rank, first_row_of(plan, phase, peer), plan.blocks)
    wait = fetch(needed, [[(keys[s], block.at[s])] for s in range(6)], sem)
    total[...] = jnp.zeros_like(total)
    queries = stack_heads(qx[start : start + rows, :], heads)
    grads = stack_heads(ox[...], heads)
    for s in range(6):

        @pl.when(needed[s])
        def _(s=s):
            wait(s)
            key, value, extra = block[s, :, :128], block[s, :, 128:256], block[s, :, 256:]
            scores = dot_nt(queries, jnp.concatenate([key, extra], axis=1))
            if s == 0:
                place = lax.broadcasted_iota(jnp.int32, scores.shape, 1)
                seats = jnp.concatenate(
                    [row_places(peer, phase, plan.chunk, (rows, 1), 0, 1)] * heads, axis=0
                )
                scores = jnp.where(place <= seats, scores, -FAR)
            probs = jnp.exp2(scores * (scale * LOG2E))
            dprobs = dot_nt(grads, jnp.concatenate([value, extra], axis=1))
            total[...] += dot_nn((probs * dprobs).astype(jnp.bfloat16), key)

    def mine(at, size):
        return jnp.concatenate(
            [
                (total[h * rows + at : h * rows + at + size, :] * scale).astype(jnp.bfloat16)
                for h in range(heads)
            ],
            axis=1,
        )

    if before:
        for ref, segments in zip(done, plan.phases[:before], strict=True):
            put_rows(plan, peer, out, segments, lambda at, size, ref=ref: ref[at : at + size, :])
        put_rows(plan, peer, out, phase, mine)
    else:
        out[...] = mine(0, rows)


def query_gradient(plan, number, docs, keys, qx, ox, done):
    rows, width = ox.shape[0], plan.heads * 128
    out_rows = sum(d.shape[0] for d in done) + rows
    vmem, any_place = pl.BlockSpec(memory_space=pltpu.VMEM), pl.BlockSpec(memory_space=pl.ANY)
    return pl.pallas_call(
        functools.partial(query_kernel, plan, number, len(done)),
        in_specs=[pl.BlockSpec(memory_space=pltpu.SMEM)] + [any_place] * 6 + [vmem] * (2 + len(done)),
        out_specs=vmem,
        out_shape=jax.ShapeDtypeStruct((out_rows, width), jnp.bfloat16),
        scratch_shapes=[
            pltpu.VMEM((plan.heads * rows, 128), jnp.float32),
            pltpu.VMEM((6, *keys[0].shape), jnp.bfloat16),
            pltpu.SemaphoreType.DMA((6,)),
        ],
        compiler_params=pltpu.CompilerParams(vmem_limit_bytes=VMEM_LIMIT),
        cost_estimate=pl.CostEstimate(flops=COST, bytes_accessed=0, transcendentals=0),
        name="query_gradient",
    )(docs, *keys, qx, ox, *done)


def key_kernel(plan, number, first, last, docs, own, *refs):
    heads, scale, phase = plan.heads, plan.scale, plan.phases[number]
    start = sum(size for p in plan.phases[1:number] for _, _, size in p)
    qxs, oxs = refs[:6], refs[6:12]
    before = refs[12:-5]
    out, total, queries_in, grads_in, sem = refs[-5:]
    rows = oxs[0].shape[0]
    rank, peer = lax.axis_index("ctx"), lax.axis_index("tp")
    core = lax.rem(rank, 2)
    first_row = first_row_of(plan, phase, peer)
    needed = []
    for s in range(6):
        step = 2 * s if s < 3 else 2 * (s - 3) - 2 * core + 1
        fits = (step >= 0) & (step <= RANKS_BACK) & (rank + step < plan.ranks)
        needed.append(reached(docs, rank, first_row, step, fits, plan.blocks, False))
    wait = fetch(
        needed,
        [
            [
                (qxs[s].at[pl.ds(start, rows)], queries_in.at[s]),
                (oxs[s], grads_in.at[s]),
            ]
            for s in range(6)
        ],
        sem,
    )
    total[...] = sum((x[...].astype(jnp.float32) for x in before), jnp.zeros_like(total))
    for s in range(6):

        @pl.when(needed[s])
        def _(s=s):
            wait(s)
            block = own[...]
            key, value, extra = block[:, :128], block[:, 128:256], block[:, 256:]
            queries = stack_heads(queries_in[s], heads)
            grads = stack_heads(grads_in[s], heads)
            scores = dot_nt(jnp.concatenate([key, extra], axis=1), queries)
            if s == 0:
                place = lax.broadcasted_iota(jnp.int32, scores.shape, 0)
                seats = row_places(peer, phase, plan.chunk, (1, heads * rows), 1, heads)
                scores = jnp.where(place <= seats, scores, -FAR)
            probs = jnp.exp2(scores * (scale * LOG2E))
            dprobs = dot_nt(jnp.concatenate([value, extra], axis=1), grads)
            total[:, :128] += scale * dot_nn(
                (probs * dprobs).astype(jnp.bfloat16), queries[:, :128]
            )
            total[:, 128:] += dot_nn(probs.astype(jnp.bfloat16), grads[:, :128])

    out[...] = total[...].astype(out.dtype)


def key_gradient(plan, number, docs, own, qxs, oxs, before, last):
    tokens, rows = own.shape[0], oxs[0].shape[0]
    vmem, any_place = pl.BlockSpec(memory_space=pltpu.VMEM), pl.BlockSpec(memory_space=pl.ANY)
    return pl.pallas_call(
        functools.partial(key_kernel, plan, number, not before, last),
        in_specs=[pl.BlockSpec(memory_space=pltpu.SMEM), vmem]
        + [any_place] * 12
        + [vmem] * len(before),
        out_specs=vmem,
        out_shape=jax.ShapeDtypeStruct((tokens, 256), jnp.bfloat16 if last else jnp.float32),
        scratch_shapes=[
            pltpu.VMEM((tokens, 256), jnp.float32),
            pltpu.VMEM((6, rows, qxs[0].shape[1]), jnp.bfloat16),
            pltpu.VMEM((6, *oxs[0].shape), jnp.bfloat16),
            pltpu.SemaphoreType.DMA((12,)),
        ],
        compiler_params=pltpu.CompilerParams(vmem_limit_bytes=VMEM_LIMIT),
        cost_estimate=pl.CostEstimate(flops=COST, bytes_accessed=0, transcendentals=0),
        name="key_gradient",
    )(docs, own, *qxs, *oxs, *before)


def shift(x, axis, by):
    peers = lax.axis_size(axis)
    return lax.ppermute(x, axis, [(i, i + by) for i in range(peers) if 0 <= i + by < peers])


def swap(x, axis, bits):
    return lax.ppermute(x, axis, [(i, i ^ bits) for i in range(lax.axis_size(axis))])


def reach_out(x, direction, relay):
    near = shift(x, "ctx", 2 * direction)
    return near, shift(near, "ctx", 2 * direction) if relay else shift(x, "ctx", 4 * direction)


def after(x, others):
    return after_all([x], others)[0]


def after_all(xs, others):
    return list(lax.optimization_barrier((*xs, *others))[: len(xs)])


class Plan(NamedTuple):
    heads: int
    kv_heads: int
    sharing: int
    chunk: int
    blocks: int
    ranks: int
    scale: float
    steps: tuple
    phases: tuple


def transfer_steps(peers, chunk):
    bits = [1 << b for b in range(peers.bit_length() - 1)]
    steps = []
    steps.append([(b, 0, chunk, b) for b in bits])
    for count in range(2, len(bits) + 1):
        size = chunk // count
        cuts = [(0, size)]
        for low, length in cuts:
            steps.append(
                [
                    (j, i * size + low, length, b)
                    for j in range(peers)
                    if j.bit_count() == count
                    for i, b in enumerate([b for b in bits if j & b])
                ]
            )
    return steps


def merged(pieces):
    joined = []
    for j, low, size in sorted(pieces):
        if joined and joined[-1][0] == j and joined[-1][1] + joined[-1][2] == low:
            joined[-1] = (j, joined[-1][1], joined[-1][2] + size)
        else:
            joined.append((j, low, size))
    return tuple(joined)


def rows_held(held, j, low, size):
    found, place = [], low
    while place < low + size:
        for (at, start, length), piece in held.items():
            if at == j and start <= place < start + length:
                stop = min(low + size, start + length)
                found.append(piece if (place, stop) == (start, start + length) else piece[place - start : stop - start])
                place = stop
                break
    return found[0] if len(found) == 1 else jnp.concatenate(found, axis=0)


def per_device(
    queries, key_tensor, value_tensor, attn_output, logsumexp_rows, grad_output, out_proj, block_doc
):
    tokens, heads, features = queries.shape
    kv_heads = key_tensor.shape[1]
    ranks, peers = lax.axis_size("ctx"), lax.axis_size("tp")
    chunk = tokens // peers
    peer = lax.axis_index("tp")
    steps = transfer_steps(peers, chunk)
    arrivals = [[(0, 0, chunk)] + [piece[:3] for piece in steps[0]]]
    arrivals += [[piece[:3] for piece in step] for step in steps[1:]]
    sharing = peers // kv_heads
    plan = Plan(
        heads, kv_heads, sharing, chunk, tokens // DOCBLK, ranks, features**-0.5, (),
        tuple(merged(pieces) for pieces in arrivals),
    )

    qx, attn, keys_own = prepare(
        plan,
        block_doc,
        queries.reshape(tokens, heads * features),
        attn_output.reshape(tokens, heads * features),
        logsumexp_rows,
        key_tensor.reshape(tokens, kv_heads * features),
        value_tensor.reshape(tokens, kv_heads * features),
    )
    held = {(0, 0, chunk): grad_output}

    def transfer(step):
        held.update(
            {
                (j, low, size): swap(rows_held(held, j ^ b, low, size), "tp", b)
                for j, low, size, b in step
            }
        )

    def projected(pieces, at):
        parts = [held[p] for p in sorted(pieces)]
        size = sum(p[2] for p in pieces)
        if any(p.shape[0] % 16 for p in parts):
            parts = [jnp.concatenate(parts, axis=0)]
        return project(parts, out_proj, attn[at : at + size], heads)

    def swapped(xs):
        return [swap(x, "ctx", 1) for x in xs]

    transfer(steps[0])
    first = projected([(0, 0, chunk)], 0)
    keys = [keys_own, *reach_out(keys_own, 1, False)]
    early = sum(p[2] for p in plan.phases[0])
    late = qx[early:]
    lates = [late, *reach_out(late, -1, False)]
    keys += swapped(after_all(keys, [lates[-1]]))
    lates += swapped(after_all(lates, [keys[-1]]))
    pieces = [p[:3] for p in steps[0]]
    for piece, rows in zip(pieces, after_all([held[p] for p in pieces], [lates[-1]]), strict=True):
        held[piece] = rows

    for step in steps[1:]:
        transfer(step)
    second = projected(pieces, chunk)
    query_part, own_part, other_part = early_gradients(plan, block_doc, keys, qx, [first, second])
    summed = own_part.astype(jnp.float32) + swap(other_part, "ctx", 1).astype(jnp.float32)
    hop = shift(summed[2].astype(jnp.bfloat16), "ctx", -2)
    hop = shift((summed[1] + hop.astype(jnp.float32)).astype(jnp.bfloat16), "ctx", -2)
    chained = summed[0] + hop.astype(jnp.float32)

    at = early
    oxs = []
    for pieces in arrivals[1:]:
        ox = projected(pieces, at)
        oxs.append([ox, *reach_out(ox, -1, False)])
        at += sum(p[2] for p in pieces)
    for i in range(len(oxs)):
        oxs[i] += swapped(oxs[i])
    total = None
    numbers = range(1, len(plan.phases))
    for i in numbers:
        last = i == numbers[-1]
        before = ([] if total is None else [total]) + ([chained] if last else [])
        total = key_gradient(plan, i, block_doc, keys_own, lates, oxs[i - 1], before, last)
    query_parts = [query_part]
    for i in numbers:
        done = query_parts if i == numbers[-1] else []
        query_parts.append(
            query_gradient(plan, i, block_doc, keys, late, after(oxs[i - 1][0], [total]), done)
        )
    grad_query = query_parts[-1].reshape(tokens, heads, features)
    group = peer // sharing

    def for_peer(j):
        return lax.dynamic_slice_in_dim(total, (peer ^ j) * chunk, chunk, 0)

    sums = []
    for own in range(kv_heads):
        terms = [
            for_peer(j) if j == 0 else swap(for_peer(j), "tp", j)
            for j in range(own * sharing, (own + 1) * sharing)
        ]
        sums.append(sum(t.astype(jnp.float32) for t in terms).astype(jnp.bfloat16))
    by_head = jnp.stack(
        [
            functools.reduce(
                lambda a, b: jnp.where(group ^ h == b[0], b[1], a), enumerate(sums), sums[0]
            )
            for h in range(kv_heads)
        ],
        axis=1,
    )
    return grad_query, by_head[:, :, :features], by_head[:, :, features:]


def solution(mesh):
    placed = (
        P("ctx", "tp", None),
        P("ctx", None, None),
        P("ctx", None, None),
        P("ctx", "tp", None),
        P("tp", "ctx"),
        P(("ctx", "tp"), None),
        P("tp", None),
        P(),
    )
    return jax.shard_map(
        per_device,
        mesh=mesh,
        in_specs=placed,
        out_specs=(
            P("ctx", "tp", None),
            P(("ctx", "tp"), None, None),
            P(("ctx", "tp"), None, None),
        ),
        check_vma=False,
    )
```

```python
import functools
from typing import NamedTuple

import jax
import jax.numpy as jnp
from jax import lax
from jax.experimental import pallas as pl
from jax.experimental.pallas import tpu as pltpu
from jax.sharding import PartitionSpec as P

DOCBLK = 128
RANKS_BACK = 4
TERMS = 3
LABELS = 16
FAR = 32768.0
COST = 1000
LOG2E = 1.4426950408889634
VMEM_LIMIT = 16 * 1024 * 1024


def dot_nt(a, b):
    return lax.dot_general(a, b, (((1,), (1,)), ((), ())), preferred_element_type=jnp.float32)


def dot_nn(a, b):
    return lax.dot_general(a, b, (((1,), (0,)), ((), ())), preferred_element_type=jnp.float32)


def split_terms(columns):
    rows = columns[0].shape[0]
    lane = lax.broadcasted_iota(jnp.int32, (rows, 128), 1)
    packed = jnp.zeros((rows, 128), jnp.float32)
    for h, rest in enumerate(columns):
        for i in range(TERMS):
            term = rest.astype(jnp.bfloat16).astype(jnp.float32)
            packed = jnp.where(lane == TERMS * h + i, term, packed)
            rest = rest - term
    return packed


def head_operand(full, head, heads):
    features = full[:, head * 128 : (head + 1) * 128]
    extra = full[:, heads * 128 :]
    lane = lax.broadcasted_iota(jnp.int32, extra.shape, 1)
    mine = ((lane >= TERMS * head) & (lane < TERMS * (head + 1))) | (lane >= TERMS * heads)
    return jnp.concatenate([features, jnp.where(mine, extra, jnp.zeros_like(extra))], axis=1)


def stack_heads(full, heads):
    return jnp.concatenate([head_operand(full, h, heads) for h in range(heads)], axis=0)


def row_places(peer, segments, chunk, shape, axis, copies):
    index = lax.broadcasted_iota(jnp.int32, shape, axis)
    place, start = index, 0
    for _ in range(copies):
        for j, low, size in segments:
            base = (peer ^ j) * chunk + low
            inside = (index >= start) & (index < start + size)
            place = jnp.where(inside, index - start + base, place)
            start += size
    return place


def prepare_kernel(
    plan, docs, query, attn, lse, key, value, query_out, attn_out, key_out, packed
):
    heads, kv_heads, chunk, scale = plan.heads, plan.kv_heads, plan.chunk, plan.scale
    tokens, width = query.shape
    rank, peer = lax.axis_index("ctx"), lax.axis_index("tp")
    blocks = tokens // DOCBLK
    pad = -heads % 8
    level = lse[...] * (1.0 / scale)
    if pad:
        level = jnp.concatenate([level, jnp.zeros((pad, tokens), jnp.float32)], axis=0)
    level = level.T
    terms = split_terms([level[:, h : h + 1] for h in range(heads)])
    lane = lax.broadcasted_iota(jnp.int32, (DOCBLK, 128), 1)
    packed[:, :width] = query[...]
    for b in range(blocks):
        rows = slice(b * DOCBLK, (b + 1) * DOCBLK)
        label = TERMS * heads + lax.rem(docs[rank * blocks + b], LABELS)
        packed[rows, width:] = jnp.where(lane == label, 1.0, terms[rows]).astype(jnp.bfloat16)
    group = peer // plan.sharing
    mine = pl.ds(pl.multiple_of(group * 128, 128), 128)
    key_out[:, :128] = key[:, mine]
    key_out[:, 128:] = value[:, mine]
    start = 0
    for phase in plan.phases:
        for j, low, size in phase:
            rows = pl.ds(pl.multiple_of((peer ^ j) * chunk + low, 16), size)
            query_out[start : start + size, :] = packed[rows, :]
            attn_out[start : start + size, :] = attn[rows, :]
            start += size


def prepare(plan, docs, query, attn, lse, key, value):
    tokens, width = query.shape
    vmem = pl.BlockSpec(memory_space=pltpu.VMEM)
    return pl.pallas_call(
        functools.partial(prepare_kernel, plan),
        in_specs=[pl.BlockSpec(memory_space=pltpu.SMEM)] + [vmem] * 5,
        out_specs=[vmem] * 3,
        out_shape=[
            jax.ShapeDtypeStruct((tokens, width + 128), jnp.bfloat16),
            jax.ShapeDtypeStruct((tokens, width), jnp.bfloat16),
            jax.ShapeDtypeStruct((tokens, 256), jnp.bfloat16),
        ],
        scratch_shapes=[pltpu.VMEM((tokens, width + 128), jnp.bfloat16)],
        compiler_params=pltpu.CompilerParams(vmem_limit_bytes=VMEM_LIMIT),
        cost_estimate=pl.CostEstimate(flops=COST, bytes_accessed=0, transcendentals=0),
        name="prepare",
    )(docs, query, attn, lse, key, value)


def project_kernel(heads, parts, streamed, *refs):
    grads, weight, attn, out = refs[:parts], refs[parts], refs[parts + 1], refs[parts + 2]
    width, depth = weight.shape
    rows = jnp.concatenate([g[...] for g in grads], axis=0) if parts > 1 else grads[0][...]
    if streamed:
        held, total, sem = refs[parts + 3 :]
        block = depth // sem.shape[0]

        def copy(k):
            columns = pl.ds(k * block, block)
            return pltpu.make_async_copy(weight.at[:, columns], held.at[:, columns], sem.at[k])

        for k in range(sem.shape[0]):
            copy(k).start()
        total[...] = jnp.zeros_like(total)
        for k in range(sem.shape[0]):
            copy(k).wait()
            columns = slice(k * block, (k + 1) * block)
            total[...] += dot_nt(held[:, columns], rows[:, columns])
    deltas = []
    span = 2 * 128 if heads % 2 == 0 else 128
    for low in range(0, width, span):
        if streamed:
            part = total[low : low + span, :]
        else:
            part = dot_nt(weight[low : low + span, :], rows)
        part = part.T.astype(jnp.bfloat16)
        out[:, low : low + span] = part
        product = part.astype(jnp.float32) * attn[:, low : low + span].astype(jnp.float32)
        for h in range(span // 128):
            deltas.append(jnp.sum(product[:, h * 128 : (h + 1) * 128], axis=1, keepdims=True))
    out[:, width:] = split_terms(deltas).astype(jnp.bfloat16)


def project(grads, weight, attn, heads, streamed, early):
    rows = sum(g.shape[0] for g in grads)
    width, depth = weight.shape
    vmem, any_place = pl.BlockSpec(memory_space=pltpu.VMEM), pl.BlockSpec(memory_space=pl.ANY)
    blocks = 8 if depth % 1024 == 0 else 1
    scratch = [
        pltpu.VMEM(weight.shape, jnp.bfloat16),
        pltpu.VMEM((width, rows), jnp.float32),
        pltpu.SemaphoreType.DMA((blocks,)),
    ]
    return pl.pallas_call(
        functools.partial(project_kernel, heads, len(grads), streamed),
        in_specs=[vmem] * len(grads) + [any_place if streamed else vmem, vmem],
        out_specs=vmem,
        out_shape=jax.ShapeDtypeStruct((rows, width + 128), jnp.bfloat16),
        scratch_shapes=scratch if streamed else [],
        compiler_params=pltpu.CompilerParams(
            vmem_limit_bytes=3 * VMEM_LIMIT if streamed else VMEM_LIMIT
        ),
        cost_estimate=pl.CostEstimate(
            flops=COST if early else 10000000 * COST, bytes_accessed=0, transcendentals=0
        ),
        name="project",
    )(*grads, weight, attn)


def key_extra(docs, key_rank, heads, blocks):
    lane = lax.broadcasted_iota(jnp.int32, (DOCBLK, 128), 1)
    labelled = (lane >= TERMS * heads) & (lane < TERMS * heads + LABELS)
    parts = []
    for b in range(blocks):
        doc = docs[jnp.clip(key_rank * blocks + b, 0, docs.shape[0] - 1)]
        unlike = labelled & (lane != TERMS * heads + lax.rem(doc, LABELS))
        part = jnp.where(lane < TERMS * heads, -1.0, jnp.where(unlike, -FAR, 0.0))
        parts.append(part.astype(jnp.bfloat16))
    return jnp.concatenate(parts, axis=0)


def reached(docs, rank, first_row, step, fits, blocks, back):
    if back:
        key_rank, query_rank = rank - step, rank
    else:
        key_rank, query_rank = rank, rank + step
    last = docs.shape[0] - 1
    key_doc = docs[jnp.clip(key_rank * blocks + blocks - 1, 0, last)]
    query_doc = docs[jnp.clip(query_rank * blocks + first_row // DOCBLK, 0, last)]
    return fits & (key_doc >= query_doc)


def first_row_of(plan, phase, peer):
    return functools.reduce(jnp.minimum, [(peer ^ j) * plan.chunk + low for j, low, _ in phase])


def put_rows(plan, peer, out, segments, source):
    at = 0
    for j, low, size in segments:
        place = pl.ds(pl.multiple_of((peer ^ j) * plan.chunk + low, 16), size)
        out[place, :] = source(at, size)
        at += size


def fetch(needed, pairs, sem):
    def copies(s):
        return [
            pltpu.make_async_copy(x, y, sem.at[len(pairs[s]) * s + i])
            for i, (x, y) in enumerate(pairs[s])
        ]

    for s, need in enumerate(needed):

        @pl.when(need)
        def _(s=s):
            for copy in copies(s):
                copy.start()

    def wait(s):
        for copy in copies(s):
            copy.wait()

    return wait


def behind(docs, rank, first_row, blocks):
    core = lax.rem(rank, 2)
    needed = []
    steps = []
    for s in range(6):
        step = 2 * s if s < 3 else 2 * (s - 3) + 2 * core - 1
        fits = (step >= 0) & (step <= RANKS_BACK) & (rank - step >= 0)
        needed.append(reached(docs, rank, first_row, step, fits, blocks, True))
        steps.append(step)
    return needed, steps


def early_kernel(plan, parts, docs, *refs):
    heads, scale, phase = plan.heads, plan.scale, plan.phases[0]
    keys, qx, oxs = refs[:6], refs[6], refs[7 : 7 + parts]
    query_out, own_out, other_out, turned, block, sem = refs[-6:]
    rows, tokens = query_out.shape[0], keys[0].shape[0]
    rank, peer = lax.axis_index("ctx"), lax.axis_index("tp")
    needed, steps = behind(docs, rank, first_row_of(plan, phase, peer), plan.blocks)
    wait = fetch(needed, [[(keys[s], block.at[s])] for s in range(6)], sem)
    turned[...] = jnp.zeros_like(turned)
    other_out[...] = jnp.zeros_like(other_out)
    queries = stack_heads(qx[:rows, :], heads)
    grads = stack_heads(jnp.concatenate([x[...] for x in oxs], axis=0), heads)
    for s in range(6):
        out = own_out.at[s] if s < 3 else other_out.at[jnp.clip(s - 4 + lax.rem(rank, 2), 0, 1)]

        @pl.when(needed[s])
        def _(s=s, out=out):
            wait(s)
            key, value = block[s, :, :128], block[s, :, 128:]
            extra = key_extra(docs, rank - steps[s], heads, plan.blocks)
            scores = dot_nt(jnp.concatenate([key, extra], axis=1), queries)
            if s == 0:
                place = lax.broadcasted_iota(jnp.int32, scores.shape, 0)
                seats = row_places(peer, phase, plan.chunk, (1, heads * rows), 1, heads)
                scores = jnp.where(place <= seats, scores, -FAR)
            probs = jnp.exp2(scores * (scale * LOG2E))
            dprobs = dot_nt(jnp.concatenate([value, extra], axis=1), grads)
            dscores = (probs * dprobs).astype(jnp.bfloat16)
            turned[...] += dot_nn(key.T, dscores)
            out[:, :128] = (dot_nn(dscores, queries[:, :128]) * scale).astype(out.dtype)
            out[:, 128:] = dot_nn(probs.astype(jnp.bfloat16), grads[:, :128]).astype(out.dtype)

        if s < 3:

            @pl.when(jnp.logical_not(needed[s]))
            def _(out=out):
                out[...] = jnp.zeros(out.shape, out.dtype)

    for h in range(heads):
        query_out[:, h * 128 : (h + 1) * 128] = (
            (turned[:, h * rows : (h + 1) * rows] * scale).T.astype(jnp.bfloat16)
        )


def early_gradients(plan, docs, keys, qx, oxs, unread):
    rows, tokens = sum(x.shape[0] for x in oxs), keys[0].shape[0]
    vmem, any_place = pl.BlockSpec(memory_space=pltpu.VMEM), pl.BlockSpec(memory_space=pl.ANY)
    return pl.pallas_call(
        functools.partial(early_kernel, plan, len(oxs)),
        in_specs=[pl.BlockSpec(memory_space=pltpu.SMEM)] + [any_place] * 6 + [vmem] * (1 + len(oxs)) + [any_place],
        out_specs=[vmem] * 3,
        out_shape=[
            jax.ShapeDtypeStruct((rows, plan.heads * 128), jnp.bfloat16),
            jax.ShapeDtypeStruct((3, tokens, 256), jnp.bfloat16),
            jax.ShapeDtypeStruct((2, tokens, 256), jnp.bfloat16),
        ],
        scratch_shapes=[
            pltpu.VMEM((128, plan.heads * rows), jnp.float32),
            pltpu.VMEM((6, *keys[0].shape), jnp.bfloat16),
            pltpu.SemaphoreType.DMA((6,)),
        ],
        compiler_params=pltpu.CompilerParams(vmem_limit_bytes=VMEM_LIMIT),
        cost_estimate=pl.CostEstimate(flops=COST, bytes_accessed=0, transcendentals=0),
        name="early_gradients",
    )(docs, *keys, qx, *oxs, unread)


def query_kernel(plan, number, before, docs, *refs):
    heads, scale, phase = plan.heads, plan.scale, plan.phases[number]
    start = sum(size for p in plan.phases[1:number] for _, _, size in p)
    keys, (qx, ox), done = refs[:6], refs[6:8], refs[8 : 8 + before]
    out, total, block, sem = refs[8 + before :]
    rows = ox.shape[0]
    rank, peer = lax.axis_index("ctx"), lax.axis_index("tp")
    needed, steps = behind(docs, rank, first_row_of(plan, phase, peer), plan.blocks)
    wait = fetch(needed, [[(keys[s], block.at[s])] for s in range(6)], sem)
    total[...] = jnp.zeros_like(total)
    queries = stack_heads(qx[start : start + rows, :], heads)
    grads = stack_heads(ox[...], heads)
    for s in range(6):

        @pl.when(needed[s])
        def _(s=s):
            wait(s)
            key, value = block[s, :, :128], block[s, :, 128:]
            extra = key_extra(docs, rank - steps[s], heads, plan.blocks)
            scores = dot_nt(queries, jnp.concatenate([key, extra], axis=1))
            if s == 0:
                place = lax.broadcasted_iota(jnp.int32, scores.shape, 1)
                seats = jnp.concatenate(
                    [row_places(peer, phase, plan.chunk, (rows, 1), 0, 1)] * heads, axis=0
                )
                scores = jnp.where(place <= seats, scores, -FAR)
            probs = jnp.exp2(scores * (scale * LOG2E))
            dprobs = dot_nt(grads, jnp.concatenate([value, extra], axis=1))
            total[...] += dot_nn((probs * dprobs).astype(jnp.bfloat16), key)

    def mine(at, size):
        return jnp.concatenate(
            [
                (total[h * rows + at : h * rows + at + size, :] * scale).astype(jnp.bfloat16)
                for h in range(heads)
            ],
            axis=1,
        )

    if before:
        for ref, segments in zip(done, plan.phases[:before], strict=True):
            put_rows(plan, peer, out, segments, lambda at, size, ref=ref: ref[at : at + size, :])
        put_rows(plan, peer, out, phase, mine)
    else:
        out[...] = mine(0, rows)


def query_gradient(plan, number, docs, keys, qx, ox, done):
    rows, width = ox.shape[0], plan.heads * 128
    out_rows = sum(d.shape[0] for d in done) + rows
    vmem, any_place = pl.BlockSpec(memory_space=pltpu.VMEM), pl.BlockSpec(memory_space=pl.ANY)
    return pl.pallas_call(
        functools.partial(query_kernel, plan, number, len(done)),
        in_specs=[pl.BlockSpec(memory_space=pltpu.SMEM)] + [any_place] * 6 + [vmem] * (2 + len(done)),
        out_specs=vmem,
        out_shape=jax.ShapeDtypeStruct((out_rows, width), jnp.bfloat16),
        scratch_shapes=[
            pltpu.VMEM((plan.heads * rows, 128), jnp.float32),
            pltpu.VMEM((6, *keys[0].shape), jnp.bfloat16),
            pltpu.SemaphoreType.DMA((6,)),
        ],
        compiler_params=pltpu.CompilerParams(vmem_limit_bytes=VMEM_LIMIT),
        cost_estimate=pl.CostEstimate(flops=COST, bytes_accessed=0, transcendentals=0),
        name="query_gradient",
    )(docs, *keys, qx, ox, *done)


def key_kernel(plan, number, first, last, docs, own, *refs):
    heads, scale, phase = plan.heads, plan.scale, plan.phases[number]
    start = sum(size for p in plan.phases[1:number] for _, _, size in p)
    qxs, oxs = refs[:6], refs[6:12]
    before = refs[12:-5]
    out, total, queries_in, grads_in, sem = refs[-5:]
    rows = oxs[0].shape[0]
    rank, peer = lax.axis_index("ctx"), lax.axis_index("tp")
    core = lax.rem(rank, 2)
    first_row = first_row_of(plan, phase, peer)
    needed = []
    for s in range(6):
        step = 2 * s if s < 3 else 2 * (s - 3) - 2 * core + 1
        fits = (step >= 0) & (step <= RANKS_BACK) & (rank + step < plan.ranks)
        needed.append(reached(docs, rank, first_row, step, fits, plan.blocks, False))
    wait = fetch(
        needed,
        [
            [
                (qxs[s].at[pl.ds(start, rows)], queries_in.at[s]),
                (oxs[s], grads_in.at[s]),
            ]
            for s in range(6)
        ],
        sem,
    )
    total[...] = sum((x[...].astype(jnp.float32) for x in before), jnp.zeros_like(total))
    for s in range(6):

        @pl.when(needed[s])
        def _(s=s):
            wait(s)
            key, value = own[:, :128], own[:, 128:]
            extra = key_extra(docs, rank, heads, plan.blocks)
            queries = stack_heads(queries_in[s], heads)
            grads = stack_heads(grads_in[s], heads)
            scores = dot_nt(jnp.concatenate([key, extra], axis=1), queries)
            if s == 0:
                place = lax.broadcasted_iota(jnp.int32, scores.shape, 0)
                seats = row_places(peer, phase, plan.chunk, (1, heads * rows), 1, heads)
                scores = jnp.where(place <= seats, scores, -FAR)
            probs = jnp.exp2(scores * (scale * LOG2E))
            dprobs = dot_nt(jnp.concatenate([value, extra], axis=1), grads)
            total[:, :128] += scale * dot_nn(
                (probs * dprobs).astype(jnp.bfloat16), queries[:, :128]
            )
            total[:, 128:] += dot_nn(probs.astype(jnp.bfloat16), grads[:, :128])

    out[...] = total[...].astype(out.dtype)


def key_gradient(plan, number, docs, own, qxs, oxs, before, last):
    tokens, rows = own.shape[0], oxs[0].shape[0]
    vmem, any_place = pl.BlockSpec(memory_space=pltpu.VMEM), pl.BlockSpec(memory_space=pl.ANY)
    return pl.pallas_call(
        functools.partial(key_kernel, plan, number, not before, last),
        in_specs=[pl.BlockSpec(memory_space=pltpu.SMEM), vmem]
        + [any_place] * 12
        + [vmem] * len(before),
        out_specs=vmem,
        out_shape=jax.ShapeDtypeStruct((tokens, 256), jnp.bfloat16 if last else jnp.float32),
        scratch_shapes=[
            pltpu.VMEM((tokens, 256), jnp.float32),
            pltpu.VMEM((6, rows, qxs[0].shape[1]), jnp.bfloat16),
            pltpu.VMEM((6, *oxs[0].shape), jnp.bfloat16),
            pltpu.SemaphoreType.DMA((12,)),
        ],
        compiler_params=pltpu.CompilerParams(vmem_limit_bytes=VMEM_LIMIT),
        cost_estimate=pl.CostEstimate(flops=COST, bytes_accessed=0, transcendentals=0),
        name="key_gradient",
    )(docs, own, *qxs, *oxs, *before)


def shift(x, axis, by):
    peers = lax.axis_size(axis)
    return lax.ppermute(x, axis, [(i, i + by) for i in range(peers) if 0 <= i + by < peers])


def swap(x, axis, bits):
    return lax.ppermute(x, axis, [(i, i ^ bits) for i in range(lax.axis_size(axis))])


def reach_out(x, direction, relay):
    near = shift(x, "ctx", 2 * direction)
    return near, shift(near, "ctx", 2 * direction) if relay else shift(x, "ctx", 4 * direction)


def after(x, others):
    return after_all([x], others)[0] if others else x


def after_all(xs, others):
    return list(lax.optimization_barrier((*xs, *others))[: len(xs)])


class Plan(NamedTuple):
    heads: int
    kv_heads: int
    sharing: int
    chunk: int
    blocks: int
    ranks: int
    scale: float
    steps: tuple
    phases: tuple


def transfer_steps(peers, chunk):
    bits = [1 << b for b in range(peers.bit_length() - 1)]
    steps = []
    steps.append([(b, 0, chunk, b) for b in bits])
    for count in range(2, len(bits) + 1):
        size = chunk // count
        cuts = [(0, size)]
        for low, length in cuts:
            steps.append(
                [
                    (j, i * size + low, length, b)
                    for j in range(peers)
                    if j.bit_count() == count
                    for i, b in enumerate([b for b in bits if j & b])
                ]
            )
    return steps


def merged(pieces):
    joined = []
    for j, low, size in sorted(pieces):
        if joined and joined[-1][0] == j and joined[-1][1] + joined[-1][2] == low:
            joined[-1] = (j, joined[-1][1], joined[-1][2] + size)
        else:
            joined.append((j, low, size))
    return tuple(joined)


def rows_held(held, j, low, size):
    found, place = [], low
    while place < low + size:
        for (at, start, length), piece in held.items():
            if at == j and start <= place < start + length:
                stop = min(low + size, start + length)
                found.append(piece if (place, stop) == (start, start + length) else piece[place - start : stop - start])
                place = stop
                break
    return found[0] if len(found) == 1 else jnp.concatenate(found, axis=0)


def per_device(
    queries, key_tensor, value_tensor, attn_output, logsumexp_rows, grad_output, out_proj, block_doc
):
    tokens, heads, features = queries.shape
    kv_heads = key_tensor.shape[1]
    ranks, peers = lax.axis_size("ctx"), lax.axis_size("tp")
    chunk = tokens // peers
    peer = lax.axis_index("tp")
    steps = transfer_steps(peers, chunk)
    single = [step for step in steps if all(p[0] == p[3] for p in step)]
    forwarded = steps[len(single) :]
    arrivals = [[(0, 0, chunk)] + [piece[:3] for step in single for piece in step]]
    for count in range(2, peers.bit_length()):
        arrivals.append([p[:3] for step in forwarded for p in step if p[0].bit_count() == count])
    sharing = peers // kv_heads
    plan = Plan(
        heads, kv_heads, sharing, chunk, tokens // DOCBLK, ranks, features**-0.5, (),
        tuple(merged(pieces) for pieces in arrivals),
    )

    qx, attn, keys_own = prepare(
        plan,
        block_doc,
        queries.reshape(tokens, heads * features),
        attn_output.reshape(tokens, heads * features),
        logsumexp_rows,
        key_tensor.reshape(tokens, kv_heads * features),
        value_tensor.reshape(tokens, kv_heads * features),
    )
    held = {(0, 0, chunk): grad_output}

    def transfer(step, gate=()):
        for j, low, size, b in step:
            rows = rows_held(held, j ^ b, low, size)
            held[j, low, size] = swap(after(rows, gate), "tp", b)
        return [held[p[:3]] for p in step]

    def projected(pieces, at, streamed=False):
        parts = [held[p] for p in sorted(pieces)]
        size = sum(p[2] for p in pieces)
        if any(p.shape[0] % 16 for p in parts):
            parts = [jnp.concatenate(parts, axis=0)]
        return project(parts, out_proj, attn[at : at + size], heads, streamed, at < sum(p[2] for p in plan.phases[0]))

    def swapped(xs):
        return [swap(x, "ctx", 1) for x in xs]

    for step in single:
        transfer(step)
    first = projected([(0, 0, chunk)], 0)
    keys = [keys_own, *reach_out(keys_own, 1, False)]
    early = sum(p[2] for p in plan.phases[0])
    late = qx[early:]
    lates = [late, *reach_out(late, -1, False)]
    keys += swapped(after_all(keys, [first, lates[-1]]))
    lates += swapped(after_all(lates, [keys[-1]]))
    pieces = arrivals[0][1:]
    for piece, rows in zip(pieces, after_all([held[p] for p in pieces], [lates[-1]]), strict=True):
        held[piece] = rows

    second = projected(pieces, chunk)
    marks = [transfer(step) for step in forwarded]
    query_part, own_part, other_part = early_gradients(
        plan, block_doc, keys, qx, [first, second], out_proj
    )
    received = swap(other_part, "ctx", 1)

    received = received.astype(jnp.float32)
    low, high = received[0], received[1]
    first_core = lax.axis_index("ctx") % 2 == 0
    shares = [jnp.where(first_core, low, 0.0), jnp.where(first_core, high, low), jnp.where(first_core, 0.0, high)]
    sums = [
        (own_part[k].astype(jnp.float32) + share).astype(jnp.bfloat16)
        for k, share in enumerate(shares)
    ]
    from_near, from_far = shift(sums[1], "ctx", -2), shift(sums[2], "ctx", -4)
    chained = [sums[0], from_near, from_far]

    at = early
    oxs = []
    for i, pieces in enumerate(arrivals[1:]):
        ox = after(projected(pieces, at, True), [from_near, from_far])
        oxs.append([ox, *reach_out(ox, -1, False)])
        at += sum(p[2] for p in pieces)
    for i in range(len(oxs)):
        gate = [] if i + 1 == len(oxs) else [oxs[-1][0]]
        oxs[i] += swapped(after_all(oxs[i], gate))
    total = None
    numbers = range(1, len(plan.phases))
    for i in numbers:
        last = i == numbers[-1]
        before = chained if total is None else [total]
        total = key_gradient(plan, i, block_doc, keys_own, lates, oxs[i - 1], before, last)
    query_parts = [query_part]
    for i in numbers:
        done = query_parts if i == numbers[-1] else []
        query_parts.append(
            query_gradient(plan, i, block_doc, keys, late, after(oxs[i - 1][0], [total]), done)
        )
    grad_query = query_parts[-1].reshape(tokens, heads, features)
    group = peer // sharing

    def for_peer(j):
        return lax.dynamic_slice_in_dim(total, (peer ^ j) * chunk, chunk, 0)

    sums = []
    for own in range(kv_heads):
        terms = [
            for_peer(j) if j == 0 else swap(for_peer(j), "tp", j)
            for j in range(own * sharing, (own + 1) * sharing)
        ]
        sums.append(sum(t.astype(jnp.float32) for t in terms).astype(jnp.bfloat16))
    by_head = jnp.stack(
        [
            functools.reduce(
                lambda a, b: jnp.where(group ^ h == b[0], b[1], a), enumerate(sums), sums[0]
            )
            for h in range(kv_heads)
        ],
        axis=1,
    )
    return grad_query, by_head[:, :, :features], by_head[:, :, features:]


def solution(mesh):
    placed = (
        P("ctx", "tp", None),
        P("ctx", None, None),
        P("ctx", None, None),
        P("ctx", "tp", None),
        P("tp", "ctx"),
        P(("ctx", "tp"), None),
        P("tp", None),
        P(),
    )
    return jax.shard_map(
        per_device,
        mesh=mesh,
        in_specs=placed,
        out_specs=(
            P("ctx", "tp", None),
            P(("ctx", "tp"), None, None),
            P(("ctx", "tp"), None, None),
        ),
        check_vma=False,
    )
```

```python
import functools
from typing import NamedTuple

import jax
import jax.numpy as jnp
from jax import lax
from jax.experimental import pallas as pl
from jax.experimental.pallas import tpu as pltpu
from jax.sharding import PartitionSpec as P

DOCBLK = 128
RANKS_BACK = 4
TERMS = 3
LABELS = 16
FAR = 32768.0
COST = 1000
LOG2E = 1.4426950408889634
VMEM_LIMIT = 16 * 1024 * 1024


def dot_nt(a, b):
    return lax.dot_general(a, b, (((1,), (1,)), ((), ())), preferred_element_type=jnp.float32)


def dot_nn(a, b):
    return lax.dot_general(a, b, (((1,), (0,)), ((), ())), preferred_element_type=jnp.float32)


def split_terms(columns):
    rows = columns[0].shape[0]
    lane = lax.broadcasted_iota(jnp.int32, (rows, 128), 1)
    packed = jnp.zeros((rows, 128), jnp.float32)
    for h, rest in enumerate(columns):
        for i in range(TERMS):
            term = rest.astype(jnp.bfloat16).astype(jnp.float32)
            packed = jnp.where(lane == TERMS * h + i, term, packed)
            rest = rest - term
    return packed


def head_operand(full, head, heads):
    features = full[:, head * 128 : (head + 1) * 128]
    extra = full[:, heads * 128 :]
    lane = lax.broadcasted_iota(jnp.int32, extra.shape, 1)
    mine = ((lane >= TERMS * head) & (lane < TERMS * (head + 1))) | (lane >= TERMS * heads)
    return jnp.concatenate([features, jnp.where(mine, extra, jnp.zeros_like(extra))], axis=1)


def stack_heads(full, heads):
    return jnp.concatenate([head_operand(full, h, heads) for h in range(heads)], axis=0)


def row_places(peer, segments, chunk, shape, axis, copies):
    index = lax.broadcasted_iota(jnp.int32, shape, axis)
    place, start = index, 0
    for _ in range(copies):
        for j, low, size in segments:
            base = (peer ^ j) * chunk + low
            inside = (index >= start) & (index < start + size)
            place = jnp.where(inside, index - start + base, place)
            start += size
    return place


def prepare_kernel(
    plan, docs, query, attn, lse, key, value, query_out, attn_out, key_out, packed
):
    heads, kv_heads, chunk, scale = plan.heads, plan.kv_heads, plan.chunk, plan.scale
    tokens, width = query.shape
    rank, peer = lax.axis_index("ctx"), lax.axis_index("tp")
    blocks = tokens // DOCBLK
    pad = -heads % 8
    level = lse[...] * (1.0 / scale)
    if pad:
        level = jnp.concatenate([level, jnp.zeros((pad, tokens), jnp.float32)], axis=0)
    level = level.T
    terms = split_terms([level[:, h : h + 1] for h in range(heads)])
    lane = lax.broadcasted_iota(jnp.int32, (DOCBLK, 128), 1)
    packed[:, :width] = query[...]
    for b in range(blocks):
        rows = slice(b * DOCBLK, (b + 1) * DOCBLK)
        label = TERMS * heads + lax.rem(docs[rank * blocks + b], LABELS)
        packed[rows, width:] = jnp.where(lane == label, 1.0, terms[rows]).astype(jnp.bfloat16)
    group = peer // plan.sharing
    mine = pl.ds(pl.multiple_of(group * 128, 128), 128)
    key_out[:, :128] = key[:, mine]
    key_out[:, 128:] = value[:, mine]
    start = 0
    for phase in plan.phases:
        for j, low, size in phase:
            rows = pl.ds(pl.multiple_of((peer ^ j) * chunk + low, 16), size)
            query_out[start : start + size, :] = packed[rows, :]
            attn_out[start : start + size, :] = attn[rows, :]
            start += size


def prepare(plan, docs, query, attn, lse, key, value):
    tokens, width = query.shape
    vmem = pl.BlockSpec(memory_space=pltpu.VMEM)
    return pl.pallas_call(
        functools.partial(prepare_kernel, plan),
        in_specs=[pl.BlockSpec(memory_space=pltpu.SMEM)] + [vmem] * 5,
        out_specs=[vmem] * 3,
        out_shape=[
            jax.ShapeDtypeStruct((tokens, width + 128), jnp.bfloat16),
            jax.ShapeDtypeStruct((tokens, width), jnp.bfloat16),
            jax.ShapeDtypeStruct((tokens, 256), jnp.bfloat16),
        ],
        scratch_shapes=[pltpu.VMEM((tokens, width + 128), jnp.bfloat16)],
        compiler_params=pltpu.CompilerParams(vmem_limit_bytes=VMEM_LIMIT),
        cost_estimate=pl.CostEstimate(flops=COST, bytes_accessed=0, transcendentals=0),
        name="prepare",
    )(docs, query, attn, lse, key, value)


def project_kernel(heads, parts, streamed, *refs):
    grads, weight, attn, out = refs[:parts], refs[parts], refs[parts + 1], refs[parts + 2]
    width, depth = weight.shape
    rows = jnp.concatenate([g[...] for g in grads], axis=0) if parts > 1 else grads[0][...]
    if streamed:
        held, total, sem = refs[parts + 3 :]
        block = depth // sem.shape[0]

        def copy(k):
            columns = pl.ds(k * block, block)
            return pltpu.make_async_copy(weight.at[:, columns], held.at[:, columns], sem.at[k])

        for k in range(sem.shape[0]):
            copy(k).start()
        total[...] = jnp.zeros_like(total)
        for k in range(sem.shape[0]):
            copy(k).wait()
            columns = slice(k * block, (k + 1) * block)
            total[...] += dot_nt(held[:, columns], rows[:, columns])
    deltas = []
    span = 2 * 128 if heads % 2 == 0 else 128
    for low in range(0, width, span):
        if streamed:
            part = total[low : low + span, :]
        else:
            part = dot_nt(weight[low : low + span, :], rows)
        part = part.T.astype(jnp.bfloat16)
        out[:, low : low + span] = part
        product = part.astype(jnp.float32) * attn[:, low : low + span].astype(jnp.float32)
        for h in range(span // 128):
            deltas.append(jnp.sum(product[:, h * 128 : (h + 1) * 128], axis=1, keepdims=True))
    out[:, width:] = split_terms(deltas).astype(jnp.bfloat16)


def project(grads, weight, attn, heads, streamed, early):
    rows = sum(g.shape[0] for g in grads)
    width, depth = weight.shape
    vmem, any_place = pl.BlockSpec(memory_space=pltpu.VMEM), pl.BlockSpec(memory_space=pl.ANY)
    blocks = 8 if depth % 1024 == 0 else 1
    scratch = [
        pltpu.VMEM(weight.shape, jnp.bfloat16),
        pltpu.VMEM((width, rows), jnp.float32),
        pltpu.SemaphoreType.DMA((blocks,)),
    ]
    return pl.pallas_call(
        functools.partial(project_kernel, heads, len(grads), streamed),
        in_specs=[vmem] * len(grads) + [any_place if streamed else vmem, vmem],
        out_specs=vmem,
        out_shape=jax.ShapeDtypeStruct((rows, width + 128), jnp.bfloat16),
        scratch_shapes=scratch if streamed else [],
        compiler_params=pltpu.CompilerParams(
            vmem_limit_bytes=3 * VMEM_LIMIT if streamed else VMEM_LIMIT
        ),
        cost_estimate=pl.CostEstimate(
            flops=COST if early else 10000000 * COST, bytes_accessed=0, transcendentals=0
        ),
        name="project",
    )(*grads, weight, attn)


def key_extra(docs, key_rank, heads, blocks):
    lane = lax.broadcasted_iota(jnp.int32, (DOCBLK, 128), 1)
    labelled = (lane >= TERMS * heads) & (lane < TERMS * heads + LABELS)
    parts = []
    for b in range(blocks):
        doc = docs[jnp.clip(key_rank * blocks + b, 0, docs.shape[0] - 1)]
        unlike = labelled & (lane != TERMS * heads + lax.rem(doc, LABELS))
        part = jnp.where(lane < TERMS * heads, -1.0, jnp.where(unlike, -FAR, 0.0))
        parts.append(part.astype(jnp.bfloat16))
    return jnp.concatenate(parts, axis=0)


def reached(docs, rank, first_row, step, fits, blocks, back):
    if back:
        key_rank, query_rank = rank - step, rank
    else:
        key_rank, query_rank = rank, rank + step
    last = docs.shape[0] - 1
    key_doc = docs[jnp.clip(key_rank * blocks + blocks - 1, 0, last)]
    query_doc = docs[jnp.clip(query_rank * blocks + first_row // DOCBLK, 0, last)]
    return fits & (key_doc >= query_doc)


def first_row_of(plan, phase, peer):
    return functools.reduce(jnp.minimum, [(peer ^ j) * plan.chunk + low for j, low, _ in phase])


def put_rows(plan, peer, out, segments, source):
    at = 0
    for j, low, size in segments:
        place = pl.ds(pl.multiple_of((peer ^ j) * plan.chunk + low, 16), size)
        out[place, :] = source(at, size)
        at += size


def fetch(needed, pairs, sem):
    def copies(s):
        return [
            pltpu.make_async_copy(x, y, sem.at[len(pairs[s]) * s + i])
            for i, (x, y) in enumerate(pairs[s])
        ]

    for s, need in enumerate(needed):

        @pl.when(need)
        def _(s=s):
            for copy in copies(s):
                copy.start()

    def wait(s):
        for copy in copies(s):
            copy.wait()

    return wait


def behind(docs, rank, first_row, blocks):
    core = lax.rem(rank, 2)
    needed = []
    steps = []
    for s in range(6):
        step = 2 * s if s < 3 else 2 * (s - 3) + 2 * core - 1
        fits = (step >= 0) & (step <= RANKS_BACK) & (rank - step >= 0)
        needed.append(reached(docs, rank, first_row, step, fits, blocks, True))
        steps.append(step)
    return needed, steps


def early_kernel(plan, parts, docs, *refs):
    heads, scale, phase = plan.heads, plan.scale, plan.phases[0]
    keys, qx, oxs = refs[:6], refs[6], refs[7 : 7 + parts]
    query_out, own_out, other_out, turned, block, sem = refs[-6:]
    rows, tokens = query_out.shape[0], keys[0].shape[0]
    rank, peer = lax.axis_index("ctx"), lax.axis_index("tp")
    needed, steps = behind(docs, rank, first_row_of(plan, phase, peer), plan.blocks)
    wait = fetch(needed, [[(keys[s], block.at[s])] for s in range(6)], sem)
    turned[...] = jnp.zeros_like(turned)
    other_out[...] = jnp.zeros_like(other_out)
    queries = stack_heads(qx[:rows, :], heads)
    grads = stack_heads(jnp.concatenate([x[...] for x in oxs], axis=0), heads)
    for s in range(6):
        out = own_out.at[s] if s < 3 else other_out.at[jnp.clip(s - 4 + lax.rem(rank, 2), 0, 1)]

        @pl.when(needed[s])
        def _(s=s, out=out):
            wait(s)
            key, value = block[s, :, :128], block[s, :, 128:]
            extra = key_extra(docs, rank - steps[s], heads, plan.blocks)
            scores = dot_nt(jnp.concatenate([key, extra], axis=1), queries)
            if s == 0:
                place = lax.broadcasted_iota(jnp.int32, scores.shape, 0)
                seats = row_places(peer, phase, plan.chunk, (1, heads * rows), 1, heads)
                scores = jnp.where(place <= seats, scores, -FAR)
            probs = jnp.exp2(scores * (scale * LOG2E))
            dprobs = dot_nt(jnp.concatenate([value, extra], axis=1), grads)
            dscores = (probs * dprobs).astype(jnp.bfloat16)
            turned[...] += dot_nn(key.T, dscores)
            out[:, :128] = (dot_nn(dscores, queries[:, :128]) * scale).astype(out.dtype)
            out[:, 128:] = dot_nn(probs.astype(jnp.bfloat16), grads[:, :128]).astype(out.dtype)

        if s < 3:

            @pl.when(jnp.logical_not(needed[s]))
            def _(out=out):
                out[...] = jnp.zeros(out.shape, out.dtype)

    for h in range(heads):
        query_out[:, h * 128 : (h + 1) * 128] = (
            (turned[:, h * rows : (h + 1) * rows] * scale).T.astype(jnp.bfloat16)
        )


def early_gradients(plan, docs, keys, qx, oxs, unread):
    rows, tokens = sum(x.shape[0] for x in oxs), keys[0].shape[0]
    vmem, any_place = pl.BlockSpec(memory_space=pltpu.VMEM), pl.BlockSpec(memory_space=pl.ANY)
    return pl.pallas_call(
        functools.partial(early_kernel, plan, len(oxs)),
        in_specs=[pl.BlockSpec(memory_space=pltpu.SMEM)] + [any_place] * 6 + [vmem] * (1 + len(oxs)) + [any_place],
        out_specs=[vmem] * 3,
        out_shape=[
            jax.ShapeDtypeStruct((rows, plan.heads * 128), jnp.bfloat16),
            jax.ShapeDtypeStruct((3, tokens, 256), jnp.bfloat16),
            jax.ShapeDtypeStruct((2, tokens, 256), jnp.bfloat16),
        ],
        scratch_shapes=[
            pltpu.VMEM((128, plan.heads * rows), jnp.float32),
            pltpu.VMEM((6, *keys[0].shape), jnp.bfloat16),
            pltpu.SemaphoreType.DMA((6,)),
        ],
        compiler_params=pltpu.CompilerParams(vmem_limit_bytes=VMEM_LIMIT),
        cost_estimate=pl.CostEstimate(flops=COST, bytes_accessed=0, transcendentals=0),
        name="early_gradients",
    )(docs, *keys, qx, *oxs, unread)


def query_kernel(plan, number, before, docs, *refs):
    heads, scale, phase = plan.heads, plan.scale, plan.phases[number]
    start = sum(size for p in plan.phases[1:number] for _, _, size in p)
    keys, (qx, ox), done = refs[:6], refs[6:8], refs[8 : 8 + before]
    out, total, block, sem = refs[8 + before :]
    rows = ox.shape[0]
    rank, peer = lax.axis_index("ctx"), lax.axis_index("tp")
    needed, steps = behind(docs, rank, first_row_of(plan, phase, peer), plan.blocks)
    wait = fetch(needed, [[(keys[s], block.at[s])] for s in range(6)], sem)
    total[...] = jnp.zeros_like(total)
    queries = stack_heads(qx[start : start + rows, :], heads)
    grads = stack_heads(ox[...], heads)
    for s in range(6):

        @pl.when(needed[s])
        def _(s=s):
            wait(s)
            key, value = block[s, :, :128], block[s, :, 128:]
            extra = key_extra(docs, rank - steps[s], heads, plan.blocks)
            scores = dot_nt(queries, jnp.concatenate([key, extra], axis=1))
            if s == 0:
                place = lax.broadcasted_iota(jnp.int32, scores.shape, 1)
                seats = jnp.concatenate(
                    [row_places(peer, phase, plan.chunk, (rows, 1), 0, 1)] * heads, axis=0
                )
                scores = jnp.where(place <= seats, scores, -FAR)
            probs = jnp.exp2(scores * (scale * LOG2E))
            dprobs = dot_nt(grads, jnp.concatenate([value, extra], axis=1))
            total[...] += dot_nn((probs * dprobs).astype(jnp.bfloat16), key)

    def mine(at, size):
        return jnp.concatenate(
            [
                (total[h * rows + at : h * rows + at + size, :] * scale).astype(jnp.bfloat16)
                for h in range(heads)
            ],
            axis=1,
        )

    if before:
        for ref, segments in zip(done, plan.phases[:before], strict=True):
            put_rows(plan, peer, out, segments, lambda at, size, ref=ref: ref[at : at + size, :])
        put_rows(plan, peer, out, phase, mine)
    else:
        out[...] = mine(0, rows)


def query_gradient(plan, number, docs, keys, qx, ox, done):
    rows, width = ox.shape[0], plan.heads * 128
    out_rows = sum(d.shape[0] for d in done) + rows
    vmem, any_place = pl.BlockSpec(memory_space=pltpu.VMEM), pl.BlockSpec(memory_space=pl.ANY)
    return pl.pallas_call(
        functools.partial(query_kernel, plan, number, len(done)),
        in_specs=[pl.BlockSpec(memory_space=pltpu.SMEM)] + [any_place] * 6 + [vmem] * (2 + len(done)),
        out_specs=vmem,
        out_shape=jax.ShapeDtypeStruct((out_rows, width), jnp.bfloat16),
        scratch_shapes=[
            pltpu.VMEM((plan.heads * rows, 128), jnp.float32),
            pltpu.VMEM((6, *keys[0].shape), jnp.bfloat16),
            pltpu.SemaphoreType.DMA((6,)),
        ],
        compiler_params=pltpu.CompilerParams(vmem_limit_bytes=VMEM_LIMIT),
        cost_estimate=pl.CostEstimate(flops=COST, bytes_accessed=0, transcendentals=0),
        name="query_gradient",
    )(docs, *keys, qx, ox, *done)


def key_kernel(plan, number, first, last, docs, own, *refs):
    heads, scale, phase = plan.heads, plan.scale, plan.phases[number]
    start = sum(size for p in plan.phases[1:number] for _, _, size in p)
    qxs, oxs = refs[:6], refs[6:12]
    before = refs[12:-5]
    out, total, queries_in, grads_in, sem = refs[-5:]
    rows = oxs[0].shape[0]
    rank, peer = lax.axis_index("ctx"), lax.axis_index("tp")
    core = lax.rem(rank, 2)
    first_row = first_row_of(plan, phase, peer)
    needed = []
    for s in range(6):
        step = 2 * s if s < 3 else 2 * (s - 3) - 2 * core + 1
        fits = (step >= 0) & (step <= RANKS_BACK) & (rank + step < plan.ranks)
        needed.append(reached(docs, rank, first_row, step, fits, plan.blocks, False))
    wait = fetch(
        needed,
        [
            [
                (qxs[s].at[pl.ds(start, rows)], queries_in.at[s]),
                (oxs[s], grads_in.at[s]),
            ]
            for s in range(6)
        ],
        sem,
    )
    total[...] = sum((x[...].astype(jnp.float32) for x in before), jnp.zeros_like(total))
    for s in range(6):

        @pl.when(needed[s])
        def _(s=s):
            wait(s)
            key, value = own[:, :128], own[:, 128:]
            extra = key_extra(docs, rank, heads, plan.blocks)
            queries = stack_heads(queries_in[s], heads)
            grads = stack_heads(grads_in[s], heads)
            scores = dot_nt(jnp.concatenate([key, extra], axis=1), queries)
            if s == 0:
                place = lax.broadcasted_iota(jnp.int32, scores.shape, 0)
                seats = row_places(peer, phase, plan.chunk, (1, heads * rows), 1, heads)
                scores = jnp.where(place <= seats, scores, -FAR)
            probs = jnp.exp2(scores * (scale * LOG2E))
            dprobs = dot_nt(jnp.concatenate([value, extra], axis=1), grads)
            total[:, :128] += scale * dot_nn(
                (probs * dprobs).astype(jnp.bfloat16), queries[:, :128]
            )
            total[:, 128:] += dot_nn(probs.astype(jnp.bfloat16), grads[:, :128])

    out[...] = total[...].astype(out.dtype)


def key_gradient(plan, number, docs, own, qxs, oxs, before, last):
    tokens, rows = own.shape[0], oxs[0].shape[0]
    vmem, any_place = pl.BlockSpec(memory_space=pltpu.VMEM), pl.BlockSpec(memory_space=pl.ANY)
    return pl.pallas_call(
        functools.partial(key_kernel, plan, number, not before, last),
        in_specs=[pl.BlockSpec(memory_space=pltpu.SMEM), vmem]
        + [any_place] * 12
        + [vmem] * len(before),
        out_specs=vmem,
        out_shape=jax.ShapeDtypeStruct((tokens, 256), jnp.bfloat16 if last else jnp.float32),
        scratch_shapes=[
            pltpu.VMEM((tokens, 256), jnp.float32),
            pltpu.VMEM((6, rows, qxs[0].shape[1]), jnp.bfloat16),
            pltpu.VMEM((6, *oxs[0].shape), jnp.bfloat16),
            pltpu.SemaphoreType.DMA((12,)),
        ],
        compiler_params=pltpu.CompilerParams(vmem_limit_bytes=VMEM_LIMIT),
        cost_estimate=pl.CostEstimate(flops=COST, bytes_accessed=0, transcendentals=0),
        name="key_gradient",
    )(docs, own, *qxs, *oxs, *before)


def shift(x, axis, by):
    peers = lax.axis_size(axis)
    return lax.ppermute(x, axis, [(i, i + by) for i in range(peers) if 0 <= i + by < peers])


def swap(x, axis, bits):
    return lax.ppermute(x, axis, [(i, i ^ bits) for i in range(lax.axis_size(axis))])


def reach_out(x, direction, relay):
    near = shift(x, "ctx", 2 * direction)
    return near, shift(near, "ctx", 2 * direction) if relay else shift(x, "ctx", 4 * direction)


def after(x, others):
    return after_all([x], others)[0] if others else x


def after_all(xs, others):
    return list(lax.optimization_barrier((*xs, *others))[: len(xs)])


class Plan(NamedTuple):
    heads: int
    kv_heads: int
    sharing: int
    chunk: int
    blocks: int
    ranks: int
    scale: float
    steps: tuple
    phases: tuple


def transfer_steps(peers, chunk):
    bits = [1 << b for b in range(peers.bit_length() - 1)]
    steps = []
    steps.append([(b, 0, chunk, b) for b in bits])
    for count in range(2, len(bits) + 1):
        size = chunk // count
        cuts = [(0, size)]
        for low, length in cuts:
            steps.append(
                [
                    (j, i * size + low, length, b)
                    for j in range(peers)
                    if j.bit_count() == count
                    for i, b in enumerate([b for b in bits if j & b])
                ]
            )
    return steps


def merged(pieces):
    joined = []
    for j, low, size in sorted(pieces):
        if joined and joined[-1][0] == j and joined[-1][1] + joined[-1][2] == low:
            joined[-1] = (j, joined[-1][1], joined[-1][2] + size)
        else:
            joined.append((j, low, size))
    return tuple(joined)


def rows_held(held, j, low, size):
    found, place = [], low
    while place < low + size:
        for (at, start, length), piece in held.items():
            if at == j and start <= place < start + length:
                stop = min(low + size, start + length)
                found.append(piece if (place, stop) == (start, start + length) else piece[place - start : stop - start])
                place = stop
                break
    return found[0] if len(found) == 1 else jnp.concatenate(found, axis=0)


def per_device(
    queries, key_tensor, value_tensor, attn_output, logsumexp_rows, grad_output, out_proj, block_doc
):
    tokens, heads, features = queries.shape
    kv_heads = key_tensor.shape[1]
    ranks, peers = lax.axis_size("ctx"), lax.axis_size("tp")
    chunk = tokens // peers
    peer = lax.axis_index("tp")
    steps = transfer_steps(peers, chunk)
    single = [step for step in steps if all(p[0] == p[3] for p in step)]
    forwarded = steps[len(single) :]
    arrivals = [[(0, 0, chunk)] + [piece[:3] for step in single for piece in step]]
    for count in range(2, peers.bit_length()):
        arrivals.append([p[:3] for step in forwarded for p in step if p[0].bit_count() == count])
    sharing = peers // kv_heads
    plan = Plan(
        heads, kv_heads, sharing, chunk, tokens // DOCBLK, ranks, features**-0.5, (),
        tuple(merged(pieces) for pieces in arrivals),
    )

    qx, attn, keys_own = prepare(
        plan,
        block_doc,
        queries.reshape(tokens, heads * features),
        attn_output.reshape(tokens, heads * features),
        logsumexp_rows,
        key_tensor.reshape(tokens, kv_heads * features),
        value_tensor.reshape(tokens, kv_heads * features),
    )
    held = {(0, 0, chunk): grad_output}

    def transfer(step, gate=()):
        for j, low, size, b in step:
            rows = rows_held(held, j ^ b, low, size)
            held[j, low, size] = swap(after(rows, gate), "tp", b)
        return [held[p[:3]] for p in step]

    def projected(pieces, at, streamed=False):
        parts = [held[p] for p in sorted(pieces)]
        size = sum(p[2] for p in pieces)
        if any(p.shape[0] % 16 for p in parts):
            parts = [jnp.concatenate(parts, axis=0)]
        return project(parts, out_proj, attn[at : at + size], heads, streamed, at < sum(p[2] for p in plan.phases[0]))

    def swapped(xs):
        return [swap(x, "ctx", 1) for x in xs]

    for step in single:
        transfer(step)
    first = projected([(0, 0, chunk)], 0)
    keys = [keys_own, *reach_out(keys_own, 1, False)]
    early = sum(p[2] for p in plan.phases[0])
    late = qx[early:]
    lates = [late, *reach_out(late, -1, False)]
    keys += swapped(after_all(keys, [first, lates[-1]]))
    lates += swapped(after_all(lates, [keys[-1]]))
    pieces = arrivals[0][1:]
    for piece, rows in zip(pieces, after_all([held[p] for p in pieces], [lates[-1]]), strict=True):
        held[piece] = rows

    second = projected(pieces, chunk)
    marks = [transfer(step) for step in forwarded]
    query_part, own_part, other_part = early_gradients(
        plan, block_doc, keys, qx, [first, second], out_proj
    )
    received = swap(other_part, "ctx", 1)

    received = received.astype(jnp.float32)
    low, high = received[0], received[1]
    first_core = lax.axis_index("ctx") % 2 == 0
    shares = [jnp.where(first_core, low, 0.0), jnp.where(first_core, high, low), jnp.where(first_core, 0.0, high)]
    sums = [
        (own_part[k].astype(jnp.float32) + share).astype(jnp.bfloat16)
        for k, share in enumerate(shares)
    ]
    from_near, from_far = shift(sums[1], "ctx", -2), shift(sums[2], "ctx", -4)
    chained = [sums[0], from_near, from_far]

    at = early
    oxs = []
    for i, pieces in enumerate(arrivals[1:]):
        ox = after(projected(pieces, at, True), [from_far])
        oxs.append([ox, *reach_out(ox, -1, False)])
        at += sum(p[2] for p in pieces)
    for i in range(len(oxs)):
        gate = [] if i + 1 == len(oxs) else [oxs[-1][0]]
        oxs[i] += swapped(after_all(oxs[i], gate))
    total = None
    numbers = range(1, len(plan.phases))
    for i in numbers:
        last = i == numbers[-1]
        before = chained if total is None else [total]
        total = key_gradient(plan, i, block_doc, keys_own, lates, oxs[i - 1], before, last)
    query_parts = [query_part]
    for i in numbers:
        done = query_parts if i == numbers[-1] else []
        query_parts.append(
            query_gradient(plan, i, block_doc, keys, late, after(oxs[i - 1][0], [total]), done)
        )
    grad_query = query_parts[-1].reshape(tokens, heads, features)
    group = peer // sharing

    def for_peer(j):
        return lax.dynamic_slice_in_dim(total, (peer ^ j) * chunk, chunk, 0)

    sums = []
    for own in range(kv_heads):
        terms = [
            for_peer(j) if j == 0 else swap(for_peer(j), "tp", j)
            for j in range(own * sharing, (own + 1) * sharing)
        ]
        sums.append(sum(t.astype(jnp.float32) for t in terms).astype(jnp.bfloat16))
    by_head = jnp.stack(
        [
            functools.reduce(
                lambda a, b: jnp.where(group ^ h == b[0], b[1], a), enumerate(sums), sums[0]
            )
            for h in range(kv_heads)
        ],
        axis=1,
    )
    return grad_query, by_head[:, :, :features], by_head[:, :, features:]


def solution(mesh):
    placed = (
        P("ctx", "tp", None),
        P("ctx", None, None),
        P("ctx", None, None),
        P("ctx", "tp", None),
        P("tp", "ctx"),
        P(("ctx", "tp"), None),
        P("tp", None),
        P(),
    )
    return jax.shard_map(
        per_device,
        mesh=mesh,
        in_specs=placed,
        out_specs=(
            P("ctx", "tp", None),
            P(("ctx", "tp"), None, None),
            P(("ctx", "tp"), None, None),
        ),
        check_vma=False,
    )
```
